128 devices in a mesh: dp: 32 (over z, y, core), head: 2 (over x_hi), pos: 2 (over x_lo).
Axes of the slice: x: 4 (x_hi: 2, x_lo: 2; x = x_hi * 2 + x_lo), y: 4, z: 4, core: 2. Of those that a mesh axis runs over, the one named last changes fastest.
Arguments:
- queries: bfloat16 [768, 128, 1024], P('dp', 'pos', 'head'), may hold values from -28 to 28
- output_gradient: bfloat16 [768, 128, 1024], P('dp', 'pos', 'head'), may hold values from -24 to 24
- prefix_keys: bfloat16 [32, 256, 256], P('dp', 'pos', 'head'), may hold values from -12 to 12
- prefix_values: bfloat16 [32, 256, 256], P('dp', 'pos', 'head'), may hold values from -6 to 6
- tile_prefix: int32 [768, 1], replicated, may hold values from 0 to 31; in each aligned block of 24 rows (0 to 23, 24 to 47, ...) at most 2 rows name the same one
- suffix_lse: float32 [768, 128, 8], P(None, None, 'head'), may hold values from 5 to 12
- suffix_dot: float32 [768, 128, 8], P(None, None, 'head'), may hold values from -64 to 64
Outputs:
- query_grad: bfloat16 [768, 128, 1024], P('dp', 'pos', 'head')
- key_grad: bfloat16 [32, 256, 256], P('dp', 'pos', 'head')
- value_grad: bfloat16 [32, 256, 256], P('dp', 'pos', 'head')
The draws below stay inside these ranges and needn't reach their ends.
Inputs may be any that keep to these rules, and one draw needn't show every extreme that they name: `tile_prefix`: in each aligned block of 24 tiles (the tiles of one dp index) no prefix is named by more than 2 tiles, and some block has a prefix named exactly 2 times.
All inputs are finite; a program needn't handle non-finite values.
Results may differ from the reference program's by a relative error of at most 0.012.
Values may be sent and summed in bfloat16 or wider, within the bound.
No kernel may reach another device: no remote copies, remote signals or barrier semaphores. Data moves between devices by JAX's collectives and lax.ppermute only.
A program may use at most 128 MiB of HBM per device.

```python
import math
import jax
import jax.numpy as jnp
import numpy as np
from jax import lax

HEAD_DIM = 128
Q_GROUP = 4
TILE_ROWS = 128
TILES_DP = 24
KV_HEADS = 2
HEADS = 8
PREFIX_LEN = 256
PREFIXES = 32
CAPACITY = 2
TILES = 768


def draw_queries(key, part):
    key = jax.random.fold_in(key, 11)
    full_shape = (TILES, TILE_ROWS, KV_HEADS * Q_GROUP * HEAD_DIM)
    return (2.0 * jnp.clip(jax.random.normal(key, full_shape, jnp.float32), -6.0, 6.0)).astype(jnp.bfloat16)


def draw_prefix_keys(key, part):
    key = jax.random.fold_in(key, 23)
    full_shape = (PREFIXES, PREFIX_LEN, KV_HEADS * HEAD_DIM)
    return jnp.clip(jax.random.normal(key, full_shape, jnp.float32), -6.0, 6.0).astype(jnp.bfloat16)


def levels(key, dims, cuts, least, high):
    loudness, own = 1.0, jax.random.fold_in(key, 6)
    for dim, shards_of in cuts:
        steps = jnp.exp(jax.random.uniform(jax.random.fold_in(own, dim), (shards_of,), jnp.float32, least / len(cuts), high / len(cuts)))
        loudness = loudness * jnp.repeat(steps, dims[dim] // shards_of).reshape([-1 if axis == dim else 1 for axis in range(len(dims))])
    return loudness


def shared_out(key, own, number, rows, count, top, bound, slope):
    ranking = jax.random.permutation(key, count)
    packed, ordinary = shares(count, rows * top, bound, slope, True), shares(count, rows * top, bound, slope, False)
    places = jnp.arange(count)

    def named(sizes, turn):
        used = int((sizes > 0).sum())
        fixed = max(1, used // 4)
        moved = fixed + (places - fixed + turn * (used - fixed)) % max(1, count - fixed)
        return jnp.zeros((count,), jnp.int32).at[ranking[jnp.where(places < fixed, places, moved)]].set(jnp.asarray(sizes, jnp.int32))

    sizes = jnp.where(number % 4 == 0, named(packed, number // 4), named(ordinary, number - number // 4 - 1))
    mixed = jax.random.permutation(jax.random.fold_in(own, 3), count)
    source_of, sink = mixed[0:count // 2 * 2:2], mixed[1:count // 2 * 2:2]
    margin = jnp.minimum(sizes[source_of] - 1, bound - sizes[sink]) // 2
    margin = jnp.where((source_of == ranking[0]) | (sink == ranking[0]) | (sizes[sink] == 0), 0, jnp.maximum(margin, 0))
    moved = jax.random.randint(jax.random.fold_in(own, 4), (count // 2,), 0, 1 << 20) % (margin + 1)
    sizes = sizes.at[source_of].add(-moved).at[sink].add(moved)
    members = jnp.searchsorted(jnp.cumsum(sizes), jnp.arange(rows * top), side="right").astype(jnp.int32)
    table = members.reshape(top, rows).T
    table = table[jax.random.permutation(jax.random.fold_in(own, 1), rows)]
    turn = jax.random.randint(jax.random.fold_in(own, 2), (rows, 1), 0, top)
    return jnp.take_along_axis(table, (jnp.arange(top)[None, :] + turn) % top, axis=1)


def shares(amount, total, most, slope, full):
    loads = [(1 << 20) // math.isqrt(standing ** slope) + 1 for standing in range(1, amount + 1)]
    largest = most if full else min(most, max(-(-total // amount), total * loads[0] // sum(loads)))
    least = 1 if total - largest >= amount - 1 else 0
    holding, rest = [largest] + [least] * (amount - 1), total - largest - least * (amount - 1)
    while rest > 0:
        free = [i for i in range(1, amount) if holding[i] < largest] or [i for i in range(1, amount) if holding[i] < most]
        pool, remaining = sum([loads[i] for i in free]), rest
        for i in free:
            addition = min(most - holding[i], max(1, remaining * loads[i] // pool), rest)
            holding[i] = holding[i] + addition
            rest = rest - addition
    return np.array(holding)


def gaussian(own_key, shape, scale, most, shards=(), kind=jnp.bfloat16):
    entries = scale * jax.random.normal(own_key, shape, jnp.float32)
    if shards:
        entries = entries * levels(own_key, shape, shards, -0.22, 0.18)
    return jnp.clip(entries, -most, most).astype(kind)


def setup_inputs(seed: int = 0) -> dict:
    splits = jax.random.split(jax.random.key(seed), 8)
    queries = draw_queries(jax.random.fold_in(splits[7], 71), 0)
    output_gradient = gaussian(splits[1], (TILES, TILE_ROWS, HEADS * HEAD_DIM), 4.0, 24.0, ((0, 32), (1, 2), (2, 2)))
    prefix_keys = draw_prefix_keys(jax.random.fold_in(splits[7], 71), 0)
    prefix_values = gaussian(splits[3], (PREFIXES, PREFIX_LEN, KV_HEADS * HEAD_DIM), 1.0, 6.0, ((0, 32), (1, 2), (2, 2)))
    tile_prefix_keys = jax.random.split(jax.random.fold_in(splits[4], 1), TILES // TILES_DP)
    tile_prefix_turns = jax.random.permutation(jax.random.fold_in(splits[4], 3), TILES // TILES_DP)
    tile_prefix = jax.vmap(lambda own, number: shared_out(jax.random.fold_in(splits[4], 2), own, number, TILES_DP, PREFIXES, 1, CAPACITY, 2))(tile_prefix_keys, tile_prefix_turns).reshape((TILES, 1))
    suffix_lse = jnp.clip(5.0 + 7.0 * jax.random.uniform(splits[5], (TILES, TILE_ROWS, HEADS), jnp.float32) ** levels(splits[5], (TILES, TILE_ROWS, HEADS), ((2, 2),), -0.2, 0.2), 5.0, 12.0)
    suffix_dot = gaussian(splits[6], (TILES, TILE_ROWS, HEADS), 16.0, 64.0, ((2, 2),), jnp.float32)
    return dict(queries=queries, output_gradient=output_gradient, prefix_keys=prefix_keys, prefix_values=prefix_values, tile_prefix=tile_prefix, suffix_lse=suffix_lse, suffix_dot=suffix_dot)


def reference(queries, output_gradient, prefix_keys, prefix_values, tile_prefix, suffix_lse, suffix_dot):
    scaling = HEAD_DIM ** -0.5

    def tile_step(running, pieces):
        key_total, value_total = running
        tile_query, tile_gradient, prefix_id, lse_in, dot_in = pieces
        prefix_id = prefix_id.astype(jnp.int32)
        key_rows = lax.dynamic_index_in_dim(prefix_keys, prefix_id, 0, keepdims=False)
        value_rows = lax.dynamic_index_in_dim(prefix_values, prefix_id, 0, keepdims=False)
        query_grid = tile_query.astype(jnp.float32).reshape(TILE_ROWS, KV_HEADS, Q_GROUP, HEAD_DIM)
        grad_grid = tile_gradient.astype(jnp.float32).reshape(TILE_ROWS, KV_HEADS, Q_GROUP, HEAD_DIM)
        key_grid = key_rows.astype(jnp.float32).reshape(PREFIX_LEN, KV_HEADS, HEAD_DIM)
        value_grid = value_rows.astype(jnp.float32).reshape(PREFIX_LEN, KV_HEADS, HEAD_DIM)
        scores = jnp.einsum("rgqd,jgd->rgqj", query_grid, key_grid) * scaling
        prob_grad = jnp.einsum("rgqd,jgd->rgqj", grad_grid, value_grid)
        suffix_l = lse_in.reshape(TILE_ROWS, KV_HEADS, Q_GROUP)
        suffix_d = dot_in.reshape(TILE_ROWS, KV_HEADS, Q_GROUP)
        row_top = jnp.maximum(jnp.max(scores, axis=-1), suffix_l)
        row_mass = jnp.exp(suffix_l - row_top) + jnp.sum(jnp.exp(scores - row_top[..., None]), axis=-1)
        row_lse = row_top + jnp.log(row_mass)
        weights = jnp.exp(scores - row_lse[..., None])
        row_delta = jnp.exp(suffix_l - row_lse) * suffix_d + jnp.sum(weights * prob_grad, axis=-1)
        prob_half = weights.astype(jnp.bfloat16)
        score_grad = (weights * (prob_grad - row_delta[..., None])).astype(jnp.bfloat16)
        query_part = jnp.einsum("rgqj,jgd->rgqd", score_grad.astype(jnp.float32), key_grid) * scaling
        key_part = jnp.einsum("rgqj,rgqd->jgd", score_grad.astype(jnp.float32), query_grid) * scaling
        value_part = jnp.einsum("rgqj,rgqd->jgd", prob_half.astype(jnp.float32), grad_grid)
        key_total = key_total.at[prefix_id].add(key_part.reshape(PREFIX_LEN, KV_HEADS * HEAD_DIM))
        value_total = value_total.at[prefix_id].add(value_part.reshape(PREFIX_LEN, KV_HEADS * HEAD_DIM))
        query_out = query_part.reshape(TILE_ROWS, HEADS * HEAD_DIM).astype(jnp.bfloat16)
        return (key_total, value_total), query_out

    zero_sum = jnp.zeros((PREFIXES, PREFIX_LEN, KV_HEADS * HEAD_DIM), jnp.float32)
    (key_total, value_total), query_grad = lax.scan(
        tile_step, (zero_sum, zero_sum),
        (queries, output_gradient, tile_prefix[:, 0], suffix_lse, suffix_dot))
    return query_grad, key_total.astype(jnp.bfloat16), value_total.astype(jnp.bfloat16)
```

```python
import functools
import math

import jax
import jax.numpy as jnp
from jax import lax
from jax.experimental import pallas as pl
from jax.experimental.pallas import tpu as pltpu
from jax.sharding import PartitionSpec as P

SIDE = 4
LOG2E = math.log2(math.e)


def place(z, y, core):
    return (z % SIDE) * 2 * SIDE + (y % SIDE) * 2 + core


def ring_pairs(second, step):
    pairs = []
    for z in range(SIDE):
        for y in range(SIDE):
            for core in range(2):
                along_y = (core == 0) != second
                target = place(z, y + step, core) if along_y else place(z + step, y, core)
                pairs.append((place(z, y, core), target))
    return pairs


def core_pairs():
    return [(i, i ^ 1) for i in range(2 * SIDE * SIDE)]


def shift(x, second, step):
    return lax.ppermute(x, "dp", ring_pairs(second, step))


def swap_cores(x):
    return lax.ppermute(x, "dp", core_pairs())


def swap_pos(x):
    return lax.ppermute(x, "pos", [(0, 1), (1, 0)])


def tile_grads(query, grad, keys, values, stat, scaling):
    nt = (((1,), (1,)), ((), ()))
    tn = (((0,), (0,)), ((), ()))
    f32 = jnp.float32
    scores = lax.dot_general(keys, query, nt, preferred_element_type=f32) * (scaling * LOG2E)
    prob_grad = lax.dot_general(values, grad, nt, preferred_element_type=f32)
    suffix_l = stat[0:1] * LOG2E
    suffix_d = stat[1:2]
    top = jnp.maximum(jnp.max(scores, axis=0, keepdims=True), suffix_l)
    raised = jnp.exp2(scores - top)
    suffix_part = jnp.exp2(suffix_l - top)
    inverse = 1.0 / (jnp.sum(raised, axis=0, keepdims=True) + suffix_part)
    moment = jnp.sum(raised * prob_grad, axis=0, keepdims=True) + suffix_part * suffix_d
    delta = moment * inverse
    probs = raised * inverse
    prob_half = probs.astype(jnp.bfloat16)
    score_grad = (probs * (prob_grad - delta)).astype(jnp.bfloat16)
    query_part = lax.dot_general(score_grad, keys, tn, preferred_element_type=f32) * scaling
    key_part = jnp.dot(score_grad, query, preferred_element_type=f32) * scaling
    value_part = jnp.dot(prob_half, grad, preferred_element_type=f32)
    return query_part, key_part, value_part


def stage_kernel(groups, per_group, chained, sched, queries, grads, stats, *refs):
    blocks = refs[:groups]
    refs = refs[groups + (1 if chained else 0):]
    query_grad, sums = refs[0], refs[1:1 + groups]
    query_buf, grad_buf, out_buf, in_sem, out_sem = refs[1 + groups:]
    heads = queries.shape[2] // 128
    rows = queries.shape[1]
    scaling = 128 ** -0.5
    slots = groups * per_group

    def fetch(slot, tile):
        return (
            pltpu.make_async_copy(queries.at[tile], query_buf.at[slot], in_sem.at[slot, 0]),
            pltpu.make_async_copy(grads.at[tile], grad_buf.at[slot], in_sem.at[slot, 1]),
        )

    def give(slot, tile):
        return pltpu.make_async_copy(out_buf.at[slot], query_grad.at[tile], out_sem.at[slot])

    def each(action):
        def step(slot, _):
            for turn in range(2):
                @pl.when(sched[slot, 2] > turn)
                def _():
                    action(2 * slot + turn, sched[slot, turn])
            return 0
        lax.fori_loop(0, slots, step, 0)

    def start(slot, tile):
        for copy in fetch(slot, tile):
            copy.start()

    each(start)

    def stacked(buf, slot):
        return jnp.concatenate([buf[slot, :, h * 128:(h + 1) * 128] for h in range(heads)], axis=0)

    def one(slot, tile, keys, values):
        for copy in fetch(slot, tile):
            copy.wait()
        query_part, key_part, value_part = tile_grads(
            stacked(query_buf, slot), stacked(grad_buf, slot), keys, values, stats[tile], scaling)
        query_part = query_part.astype(jnp.bfloat16)
        for h in range(heads):
            out_buf[slot, :, h * 128:(h + 1) * 128] = query_part[h * rows:(h + 1) * rows]
        give(slot, tile).start()
        return key_part, value_part

    for group in range(groups):
        def step(i, _, group=group):
            slot = group * per_group + i
            count = sched[slot, 2]
            block, total = blocks[group], sums[group]

            def store(key_part, value_part):
                total[i, :, 0:128] = key_part.astype(jnp.bfloat16)
                total[i, :, 128:256] = value_part.astype(jnp.bfloat16)

            @pl.when(count == 0)
            def _():
                total[i] = jnp.zeros(total.shape[1:], total.dtype)

            @pl.when(count == 1)
            def _():
                store(*one(2 * slot, sched[slot, 0], block[i, :, 0:128], block[i, :, 128:256]))

            @pl.when(count == 2)
            def _():
                keys, values = block[i, :, 0:128], block[i, :, 128:256]
                first = one(2 * slot, sched[slot, 0], keys, values)
                second = one(2 * slot + 1, sched[slot, 1], keys, values)
                store(first[0] + second[0], first[1] + second[1])
            return 0
        lax.fori_loop(0, per_group, step, 0)

    each(lambda slot, tile: give(slot, tile).wait())


def stage(sched, queries, grads, stats, blocks, query_grad):
    groups, per_group = len(blocks), blocks[0].shape[0]
    tiles = groups * per_group * 2
    rows, width = queries.shape[1:]
    whole = pl.BlockSpec(memory_space=pltpu.VMEM)
    away = pl.BlockSpec(memory_space=pl.ANY)
    chained = query_grad is not None
    operands = [sched, queries, grads, stats, *blocks] + ([query_grad] if chained else [])
    return pl.pallas_call(
        functools.partial(stage_kernel, groups, per_group, chained),
        out_shape=[jax.ShapeDtypeStruct(queries.shape, queries.dtype)]
        + [jax.ShapeDtypeStruct(b.shape, b.dtype) for b in blocks],
        in_specs=[pl.BlockSpec(memory_space=pltpu.SMEM), away, away, whole]
        + [whole] * groups + ([away] if chained else []),
        out_specs=[away] + [whole] * groups,
        scratch_shapes=[
            pltpu.VMEM((tiles, rows, width), queries.dtype),
            pltpu.VMEM((tiles, rows, width), queries.dtype),
            pltpu.VMEM((tiles, rows, width), queries.dtype),
            pltpu.SemaphoreType.DMA((tiles, 2)),
            pltpu.SemaphoreType.DMA((tiles,)),
        ],
        input_output_aliases={len(operands) - 1: 0} if chained else {},
        compiler_params=pltpu.CompilerParams(vmem_limit_bytes=24 << 20),
        cost_estimate=pl.CostEstimate(
            flops=6 * 5 * 2 * 256 * 256 * 128, bytes_accessed=4 << 20, transcendentals=6 * 65536),
        name="stage",
    )(*operands)


def add(*parts):
    total = parts[0].astype(jnp.float32)
    for part in parts[1:]:
        total = total + part.astype(jnp.float32)
    return total.astype(jnp.bfloat16)


def shards(queries, output_gradient, prefix_keys, prefix_values, tile_prefix, suffix_lse, suffix_dot):
    tile_count, row_count, _ = queries.shape
    dp = lax.axis_index("dp")
    pos = lax.axis_index("pos")
    z, y, core = dp // (2 * SIDE), dp // 2 % SIDE, dp % 2

    own_half = jnp.concatenate([prefix_keys[0], prefix_values[0]], axis=1)
    own = jnp.concatenate([own_half, swap_pos(own_half)], axis=0)
    line = jnp.stack([own, shift(own, False, 1), shift(own, False, 2), shift(own, False, 3)])
    mine = [line, shift(line, True, 1), shift(line, True, 3), shift(line, True, 2)]
    order = [0, 1, 3, 2]
    theirs = [swap_cores(group) for group in mine]

    target = lax.dynamic_slice(tile_prefix[:, 0], (dp * tile_count,), (tile_count,))
    far = jnp.array(order, jnp.int32).reshape(4, 1, 1)
    near = jnp.arange(4, dtype=jnp.int32).reshape(1, 1, 4)
    held_core = (core + jnp.arange(2, dtype=jnp.int32).reshape(1, 2, 1)) % 2
    along_y = jnp.where(held_core == 0, near, far)
    along_z = jnp.where(held_core == 0, far, near)
    named = (z - along_z) % SIDE * (2 * SIDE) + (y - along_y) % SIDE * 2 + held_core
    match = named.reshape(4, 8, 1) == target
    ids = lax.broadcasted_iota(jnp.int32, match.shape, 2)
    sched = jnp.stack(
        [
            jnp.min(jnp.where(match, ids, tile_count), axis=2),
            jnp.max(jnp.where(match, ids, -1), axis=2),
            jnp.sum(match.astype(jnp.int32), axis=2),
        ],
        axis=2,
    )

    def own_rows(x):
        x = jnp.transpose(x, (0, 2, 1))
        x = lax.dynamic_slice(
            x, (dp * tile_count, 0, pos * row_count), (tile_count, x.shape[1], row_count))
        return x.reshape(tile_count, 1, -1)

    stats = jnp.concatenate([own_rows(suffix_lse), own_rows(suffix_dot)], axis=1)

    query_grad = None
    parts = []
    for turn in range(4):
        query_grad, here, there = stage(
            sched[turn], queries, output_gradient, stats, [mine[turn], theirs[turn]], query_grad)
        parts.append(add(here, swap_cores(there)))
    line_sum = add(parts[0], *[shift(parts[turn], True, -order[turn]) for turn in (1, 2, 3)])
    own_sum = add(line_sum[0], *[shift(line_sum[k], False, -k) for k in (1, 2, 3)])
    half = own_sum.shape[0] // 2
    total = add(own_sum[:half], swap_pos(own_sum[half:]))
    return query_grad, total[None, :, 0:128], total[None, :, 128:256]


def solution(mesh):
    in_specs = (
        P("dp", "pos", "head"),
        P("dp", "pos", "head"),
        P("dp", "pos", "head"),
        P("dp", "pos", "head"),
        P(),
        P(None, None, "head"),
        P(None, None, "head"),
    )
    out_specs = (P("dp", "pos", "head"), P("dp", "pos", "head"), P("dp", "pos", "head"))
    return jax.shard_map(shards, mesh=mesh, in_specs=in_specs, out_specs=out_specs, check_vma=False)
```

```python
import functools
import math

import jax
import jax.numpy as jnp
from jax import lax
from jax.experimental import pallas as pl
from jax.experimental.pallas import tpu as pltpu
from jax.sharding import PartitionSpec as P

SIDE = 4
TILES = 24
PREFIXES = 32
BATCH = 4
LOG2E = math.log2(math.e)
PLACE, TILE, MODE, COUNT, NAMED, PART = 0, 32, 64, 80, 96, 128


def place(z, y, core):
    return (z % SIDE) * 2 * SIDE + (y % SIDE) * 2 + core


def line_groups():
    groups = []
    for core in range(2):
        for other in range(SIDE):
            ring = [place(other, k, 0) if core == 0 else place(k, other, 1) for k in range(SIDE)]
            groups.append([dp * 2 + pos for dp in ring for pos in range(2)])
    return groups


def exchange_line(x):
    return lax.all_to_all(x, ("dp", "pos"), 0, 0, axis_index_groups=line_groups(), tiled=True)


def shift(x, step):
    pairs = []
    for z in range(SIDE):
        for y in range(SIDE):
            pairs.append((place(z, y, 0), place(z + step, y, 0)))
            pairs.append((place(z, y, 1), place(z, y + step, 1)))
    return lax.ppermute(x, "dp", pairs)


def swap_cores(x):
    return lax.ppermute(x, "dp", [(i, i ^ 1) for i in range(2 * SIDE * SIDE)])


def held(x):
    return pltpu.with_memory_space_constraint(x, pltpu.VMEM)


def plan_kernel(spot, target, out, ids, count):
    z, y, core = spot[0], spot[1], spot[2]

    def clear(p, _):
        count[p] = 0
        ids[2 * p] = 0
        ids[2 * p + 1] = 0
        return 0

    lax.fori_loop(0, PREFIXES, clear, 0)

    def note(t, _):
        p = target[t]
        ids[2 * p + count[p]] = t
        count[p] = count[p] + 1
        return 0

    lax.fori_loop(0, TILES, note, 0)

    def where(p):
        far_z, far_y, held_core = p // (2 * SIDE), p // 2 % SIDE, p % 2
        on_first = held_core == 0
        near = jnp.where(on_first, far_y, far_z)
        far = jnp.where(on_first, z - far_z + SIDE, y - far_y + SIDE) % SIDE
        side = (held_core + core) % 2
        late = far == 2
        rank = jnp.where(far == 3, 2, far)
        return jnp.where(late, 1, 0), jnp.where(late, side * 4 + near, side * 12 + rank * 4 + near)

    def pairs(p, ends):
        late, at = where(p)
        base = late * PART
        n = jnp.where(late == 1, ends[1], ends[0])
        out[base + NAMED + at] = count[p]
        for turn in range(2):
            out[base + PLACE + n + turn] = at
            out[base + TILE + n + turn] = ids[2 * p + turn]
        out[base + MODE + n // 2] = 1
        step = jnp.where(count[p] == 2, 2, 0)
        return ends[0] + step * (1 - late), ends[1] + step * late

    def singles(p, ends):
        late, at = where(p)
        base = late * PART
        n = jnp.where(late == 1, ends[1], ends[0])
        out[base + PLACE + n] = at
        out[base + TILE + n] = ids[2 * p]
        out[base + MODE + n // 2] = 0
        step = jnp.where(count[p] == 1, 1, 0)
        return ends[0] + step * (1 - late), ends[1] + step * late

    zero = jnp.int32(0)
    ends = lax.fori_loop(0, PREFIXES, pairs, (zero, zero))
    ends = lax.fori_loop(0, PREFIXES, singles, ends)
    for late in range(2):
        base, n = late * PART, ends[late]
        last = jnp.maximum((n + 1) // 2 - 1, 0)
        out[base + COUNT] = (n + BATCH - 1) // BATCH

        def pad(j, _, base=base, n=n, last=last):
            pair = jnp.minimum(j // 2, last)
            source = jnp.maximum(jnp.minimum(2 * pair + j % 2, n - 1), 0)
            out[base + PLACE + j] = out[base + PLACE + source]
            out[base + TILE + j] = out[base + TILE + source]
            out[base + MODE + j // 2] = out[base + MODE + pair]
            return 0

        lax.fori_loop(n, (n + BATCH - 1) // BATCH * BATCH, pad, 0)


def plan(spot, target):
    small = pl.BlockSpec(memory_space=pltpu.SMEM)
    return pl.pallas_call(
        plan_kernel,
        out_shape=jax.ShapeDtypeStruct((2 * PART,), jnp.int32),
        in_specs=[small, small],
        out_specs=small,
        scratch_shapes=[pltpu.SMEM((2 * PREFIXES,), jnp.int32), pltpu.SMEM((PREFIXES,), jnp.int32)],
        name="plan",
    )(spot, target)


def tile_grads(query, grad, keys, values, stat, scaling):
    nt = (((1,), (1,)), ((), ()))
    tn = (((0,), (0,)), ((), ()))
    f32, half = jnp.float32, jnp.bfloat16
    tiles = range(len(query))
    scores = [
        lax.dot_general(keys[k], query[k], nt, preferred_element_type=f32) * (scaling * LOG2E)
        for k in tiles
    ]
    prob_grad = [
        lax.dot_general(values[k], grad[k], nt, preferred_element_type=f32) for k in tiles
    ]
    prob_half, score_grad = [], []
    for k in tiles:
        suffix_l = stat[k][0:1] * LOG2E
        suffix_d = stat[k][1:2]
        top = jnp.maximum(jnp.max(scores[k], axis=0, keepdims=True), suffix_l)
        raised = jnp.exp2(scores[k] - top)
        suffix_part = jnp.exp2(suffix_l - top)
        inverse = 1.0 / (jnp.sum(raised, axis=0, keepdims=True) + suffix_part)
        moment = jnp.sum(raised * prob_grad[k], axis=0, keepdims=True) + suffix_part * suffix_d
        probs = raised * inverse
        prob_half.append(probs.astype(half))
        score_grad.append((probs * (prob_grad[k] - moment * inverse)).astype(half))
    parts = []
    for k in tiles:
        query_part = lax.dot_general(keys[k], score_grad[k], tn, preferred_element_type=f32)
        parts.append((
            (query_part * scaling).astype(half).T,
            jnp.dot(score_grad[k], query[k], preferred_element_type=f32) * scaling,
            jnp.dot(prob_half[k], grad[k], preferred_element_type=f32),
        ))
    return parts


def stage_kernel(late, sizes, sched, queries, grads, stats, *refs):
    blocks = refs[:len(sizes)]
    query_grad, here, there, near = refs[len(sizes) + late:]
    heads = queries.shape[2] // 128
    rows = queries.shape[1]
    scaling = 128 ** -0.5
    base = late * PART
    places = here.shape[0]
    sums = (here, there)
    spans = []
    for block, size in zip(blocks, sizes):
        spans += [(block, first) for first in range(0, size, 2)]

    def clear(i, _):
        for side in range(2):
            @pl.when(sched[base + NAMED + side * places + i] == 0)
            def _():
                sums[side][i] = jnp.zeros(here.shape[1:], here.dtype)
        return 0

    lax.fori_loop(0, places, clear, 0)

    def stacked(buf, tile):
        return jnp.concatenate(
            [buf[tile, :, h * 128:(h + 1) * 128] for h in range(heads)], axis=0)

    def step(batch, _):
        at = [sched[base + PLACE + batch * BATCH + k] for k in range(BATCH)]
        tile = [sched[base + TILE + batch * BATCH + k] for k in range(BATCH)]
        mode = [sched[base + MODE + batch * (BATCH // 2) + k] for k in range(BATCH // 2)]
        for k in range(BATCH):
            for side in range(2):
                half = len(spans) // 2

                @pl.when(at[k] // places == side)
                def _():
                    for span in range(half):
                        block, first = spans[side * half + span]

                        @pl.when(at[k] % places // 2 == span)
                        def _():
                            near[k] = block[first + at[k] % 2]

        parts = tile_grads(
            [stacked(queries, t) for t in tile], [stacked(grads, t) for t in tile],
            [near[k, :, 0:128] for k in range(BATCH)], [near[k, :, 128:256] for k in range(BATCH)],
            [stats[t] for t in tile], scaling)
        for k in range(BATCH):
            for h in range(heads):
                query_grad[tile[k], :, h * 128:(h + 1) * 128] = parts[k][0][h * rows:(h + 1) * rows]

        def store(spot, key_part, value_part):
            for side in range(2):
                @pl.when(spot // places == side)
                def _():
                    sums[side][spot % places, :, 0:128] = key_part.astype(here.dtype)
                    sums[side][spot % places, :, 128:256] = value_part.astype(here.dtype)

        for pair in range(BATCH // 2):
            a, b = 2 * pair, 2 * pair + 1

            @pl.when(mode[pair] == 1)
            def _():
                store(at[a], parts[a][1] + parts[b][1], parts[a][2] + parts[b][2])

            @pl.when(mode[pair] == 0)
            def _():
                store(at[a], *parts[a][1:])
                store(at[b], *parts[b][1:])
        return 0

    lax.fori_loop(0, sched[base + COUNT], step, 0)


def stage(late, sched, queries, grads, stats, blocks, query_grad):
    sizes = tuple(block.shape[0] for block in blocks)
    places = sum(sizes) // 2
    kind = blocks[0].dtype
    block_shape = blocks[0].shape[1:]
    whole = pl.BlockSpec(memory_space=pltpu.VMEM)
    operands = [queries, grads, stats, *blocks] + ([query_grad] if late else [])
    tiles = TILES * places // (PREFIXES // 2)
    return pl.pallas_call(
        functools.partial(stage_kernel, late, sizes),
        out_shape=[
            pltpu.VMEM(queries.shape, kind),
            pltpu.VMEM((places, *block_shape), kind),
            pltpu.VMEM((places, *block_shape), kind),
        ],
        in_specs=[pl.BlockSpec(memory_space=pltpu.SMEM)] + [whole] * len(operands),
        out_specs=[whole] * 3,
        scratch_shapes=[pltpu.VMEM((BATCH, *block_shape), kind)],
        input_output_aliases={len(operands): 0} if late else {},
        compiler_params=pltpu.CompilerParams(vmem_limit_bytes=16 << 20),
        cost_estimate=pl.CostEstimate(
            flops=tiles * 10 * 256 * 256 * 128, bytes_accessed=0, transcendentals=tiles * 65536),
        name="late_stage" if late else "early_stage",
    )(sched, *[held(x) for x in operands])


def add(*parts):
    total = parts[0].astype(jnp.float32)
    for part in parts[1:]:
        total = total + part.astype(jnp.float32)
    return total.astype(jnp.bfloat16)


def shards(queries, output_gradient, prefix_keys, prefix_values, tile_prefix, suffix_lse, suffix_dot):
    tile_count, row_count, _ = queries.shape
    dp = lax.axis_index("dp")
    pos = lax.axis_index("pos")

    own = jnp.concatenate([prefix_keys[0], prefix_values[0]], axis=1)
    line = exchange_line(jnp.broadcast_to(own, (2 * SIDE, *own.shape))).reshape(SIDE, 256, 256)
    low, high = line[0:2], line[2:4]
    up_low = shift(low, 1)
    down_high = shift(high, -1)
    up_high = shift(high, 1)
    down_low = shift(low, -1)
    far_low = shift(up_low, 1)
    far_high = shift(down_high, -1)
    early = [line, up_low, up_high, down_low, down_high]
    late = [far_low, far_high]
    early = early + [swap_cores(x) for x in early]
    late = late + [swap_cores(x) for x in late]

    target = lax.dynamic_slice(tile_prefix[:, 0], (dp * tile_count,), (tile_count,))
    spot = jnp.stack([dp // (2 * SIDE), dp // 2 % SIDE, dp % 2]).astype(jnp.int32)
    sched = plan(spot, target)

    def own_rows(x):
        x = jnp.transpose(x, (0, 2, 1))
        x = lax.dynamic_slice(
            x, (dp * tile_count, 0, pos * row_count), (tile_count, x.shape[1], row_count))
        return x.reshape(tile_count, 1, -1)

    stats = jnp.concatenate([own_rows(suffix_lse), own_rows(suffix_dot)], axis=1)

    query_grad, here, there = stage(0, sched, queries, output_gradient, stats, early, None)
    back = swap_cores(there)
    query_grad, far_here, far_there = stage(
        1, sched, queries, output_gradient, stats, late, query_grad)
    far_back = swap_cores(far_there)
    from_up = shift(add(here[6:8], back[6:8]), -1)
    from_down = shift(add(here[8:10], back[8:10]), 1)
    via_down = shift(add(far_here[0:2], far_back[0:2]), -1)
    via_up = shift(add(far_here[2:4], far_back[2:4]), 1)
    rest_up = shift(add(here[4:6], back[4:6], via_down), -1)
    rest_down = shift(add(here[10:12], back[10:12], via_up), 1)
    line_sum = jnp.concatenate([
        add(here[0:2], back[0:2], rest_up, from_down),
        add(here[2:4], back[2:4], from_up, rest_down),
    ])
    total = add(*exchange_line(line_sum.reshape(2 * SIDE, *own.shape)))
    return query_grad, total[None, :, 0:128], total[None, :, 128:256]


def solution(mesh):
    in_specs = (
        P("dp", "pos", "head"),
        P("dp", "pos", "head"),
        P("dp", "pos", "head"),
        P("dp", "pos", "head"),
        P(),
        P(None, None, "head"),
        P(None, None, "head"),
    )
    out_specs = (P("dp", "pos", "head"), P("dp", "pos", "head"), P("dp", "pos", "head"))
    return jax.shard_map(shards, mesh=mesh, in_specs=in_specs, out_specs=out_specs, check_vma=False)
```

```python
import functools
import math

import jax
import jax.numpy as jnp
from jax import lax
from jax.experimental import pallas as pl
from jax.experimental.pallas import tpu as pltpu
from jax.sharding import PartitionSpec as P

SIDE = 4
TILES = 24
STAGES = 3
BATCH = 4
LOG2E = math.log2(math.e)
PLACE, TILE, MODE, COUNT, PART = 0, 1, 2, 3, 8


def place(z, y, core):
    return (z % SIDE) * 2 * SIDE + (y % SIDE) * 2 + core


def line_groups():
    groups = []
    for core in range(2):
        for other in range(SIDE):
            ring = [place(other, k, 0) if core == 0 else place(k, other, 1) for k in range(SIDE)]
            groups.append([dp * 2 + pos for dp in ring for pos in range(2)])
    return groups


def exchange_line(x):
    return lax.all_to_all(x, ("dp", "pos"), 0, 0, axis_index_groups=line_groups(), tiled=True)


def shift(x, step):
    pairs = []
    for z in range(SIDE):
        for y in range(SIDE):
            pairs.append((place(z, y, 0), place(z + step, y, 0)))
            pairs.append((place(z, y, 1), place(z, y + step, 1)))
    return lax.ppermute(x, "dp", pairs)


def swap_cores(x):
    return lax.ppermute(x, "dp", [(i, i ^ 1) for i in range(2 * SIDE * SIDE)])


def held(x):
    return pltpu.with_memory_space_constraint(x, pltpu.VMEM)


def distant(x):
    return pltpu.with_memory_space_constraint(x, pltpu.HBM)


def spread_kernel(keys, values, out, both, sem):
    both[:, 0:128] = keys[0]
    both[:, 128:256] = values[0]
    copies = [
        pltpu.make_async_copy(both, out.at[k], sem.at[k]) for k in range(out.shape[0])]
    for copy in copies:
        copy.start()
    for copy in copies:
        copy.wait()


def spread(keys, values):
    whole = pl.BlockSpec(memory_space=pltpu.VMEM)
    return pl.pallas_call(
        spread_kernel,
        out_shape=jax.ShapeDtypeStruct((2 * SIDE, keys.shape[1], 256), keys.dtype),
        in_specs=[whole, whole],
        out_specs=pl.BlockSpec(memory_space=pl.ANY),
        scratch_shapes=[
            pltpu.VMEM((keys.shape[1], 256), keys.dtype),
            pltpu.SemaphoreType.DMA((2 * SIDE,)),
        ],
        name="spread",
    )(keys, values)


def plan_kernel(code_ref, out):
    shape = (TILES, 128)
    lane = lax.broadcasted_iota(jnp.int32, shape, 1)
    row = lax.broadcasted_iota(jnp.int32, shape, 0)
    code = jnp.broadcast_to(code_ref[...], shape)
    mine = jnp.sum(jnp.where(lane == row, code, 0), axis=1, keepdims=True)
    code = jnp.where(lane < TILES, code, -1)
    twin = (code >> 10 == mine >> 10) & (lane != row)
    dup = jnp.sum(twin.astype(jnp.int32), axis=1, keepdims=True)
    stage = mine >> 8 & 3
    at = mine & 255
    key = stage * 4096 + (1 - dup) * 2048 + at * 32 + row[:, 0:1]
    keys = jnp.sum(jnp.where(lane == row, key, 0), axis=0, keepdims=True)
    ahead = (keys < key) & (keys >> 12 == stage) & (lane < TILES)
    rank = jnp.sum(ahead.astype(jnp.int32), axis=1, keepdims=True)
    for turn in range(STAGES):
        here = stage == turn
        n = jnp.sum(jnp.where(here & (lane == 0), 1, 0))
        last = jnp.maximum((n + 1) // 2 - 1, 0)
        pair = jnp.minimum(lane // 2, last)
        source = jnp.maximum(jnp.minimum(2 * pair + lane % 2, n - 1), 0)
        picked = here & (rank == source)
        first = PART * turn

        def put(line, value, chosen):
            out[first + line:first + line + 1, :] = jnp.sum(
                jnp.where(chosen, value, 0), axis=0, keepdims=True)

        put(PLACE, at, picked)
        put(TILE, row, picked)
        put(MODE, dup, picked)
        out[first + COUNT:first + COUNT + 1, :] = jnp.full((1, 128), (n + BATCH - 1) // BATCH)


def plan(code):
    whole = pl.BlockSpec(memory_space=pltpu.VMEM)
    return pl.pallas_call(
        plan_kernel,
        out_shape=pltpu.VMEM((STAGES * PART, 128), jnp.int32),
        in_specs=[whole],
        out_specs=whole,
        name="plan",
    )(code)


def tile_grads(query, grad, keys, values, stat, scaling):
    nt = (((1,), (1,)), ((), ()))
    tn = (((0,), (0,)), ((), ()))
    f32, half = jnp.float32, jnp.bfloat16
    tiles = range(len(query))
    scores = [
        lax.dot_general(keys[k], query[k], nt, preferred_element_type=f32) * (scaling * LOG2E)
        for k in tiles
    ]
    prob_grad = [
        lax.dot_general(values[k], grad[k], nt, preferred_element_type=f32) for k in tiles
    ]
    prob_half, score_grad = [], []
    for k in tiles:
        suffix_l = stat[k][0:1] * LOG2E
        suffix_d = stat[k][1:2]
        top = jnp.maximum(jnp.max(scores[k], axis=0, keepdims=True), suffix_l)
        raised = jnp.exp2(scores[k] - top)
        suffix_part = jnp.exp2(suffix_l - top)
        inverse = 1.0 / (jnp.sum(raised, axis=0, keepdims=True) + suffix_part)
        moment = jnp.sum(raised * prob_grad[k], axis=0, keepdims=True) + suffix_part * suffix_d
        probs = raised * inverse
        prob_half.append(probs.astype(half))
        score_grad.append((probs * (prob_grad[k] - moment * inverse)).astype(half))
    parts = []
    for k in tiles:
        query_part = lax.dot_general(keys[k], score_grad[k], tn, preferred_element_type=f32)
        parts.append((
            (query_part * scaling).astype(half).T,
            jnp.dot(score_grad[k], query[k], preferred_element_type=f32) * scaling,
            jnp.dot(prob_half[k], grad[k], preferred_element_type=f32),
        ))
    return parts


def stage_kernel(turn, sizes, sched, *refs):
    if turn == 0:
        queries, grads, stats, *blocks = refs[:3 + len(sizes)]
        query_grad, sums, there, tile_rows, near, arrived = refs[3 + len(sizes):]
    else:
        tile_rows, stats, *blocks = refs[:2 + len(sizes)]
        query_grad, sums, there, *result, near, arrived = refs[3 + len(sizes):]
    _, _, rows, width = tile_rows.shape
    heads = width // 128
    scaling = 128 ** -0.5
    base = turn * PART
    places = sums.shape[0]
    count = sched[base + COUNT, 0]
    loads, first = [], 0
    for block, size in zip(blocks, sizes):
        loads.append(pltpu.make_async_copy(
            block, near.at[first:first + size], arrived.at[len(loads)]))
        first += size
    if turn == 0:
        for which, source in enumerate((queries, grads)):
            loads.append(pltpu.make_async_copy(
                source, tile_rows.at[which], arrived.at[len(loads)]))
    for load in loads:
        load.start()
    sums[...] = jnp.zeros(sums.shape, sums.dtype)
    for load in loads:
        load.wait()

    def stacked(which, tile):
        return jnp.concatenate(
            [tile_rows[which, tile, :, h * 128:(h + 1) * 128] for h in range(heads)], axis=0)

    def step(batch, _):
        at = [sched[base + PLACE, batch * BATCH + k] for k in range(BATCH)]
        tile = [sched[base + TILE, batch * BATCH + k] for k in range(BATCH)]
        twins = [sched[base + MODE, batch * BATCH + 2 * pair] for pair in range(BATCH // 2)]
        parts = tile_grads(
            [stacked(0, t) for t in tile], [stacked(1, t) for t in tile],
            [near[k, :, 0:128] for k in at], [near[k, :, 128:256] for k in at],
            [stats[t] for t in tile], scaling)
        for k in range(BATCH):
            for h in range(heads):
                query_grad[tile[k], :, h * 128:(h + 1) * 128] = parts[k][0][h * rows:(h + 1) * rows]
        for pair in range(BATCH // 2):
            a, b = 2 * pair, 2 * pair + 1
            other = jnp.where(twins[pair] == 1, 1.0, 0.0)
            for one, two in ((a, b), (b, a)):
                for part in (1, 2):
                    sums[at[one], :, part * 128 - 128:part * 128] = (
                        parts[one][part] + other * parts[two][part]).astype(sums.dtype)
        return 0

    lax.fori_loop(0, count, step, 0)
    handed = pltpu.make_async_copy(sums.at[places // 2:places], there, arrived.at[0])
    handed.start()
    if turn == STAGES - 1:
        final = pltpu.make_async_copy(query_grad, result[0], arrived.at[1])
        final.start()
        final.wait()
    handed.wait()


def stage(turn, sched, tile_rows, stats, blocks, query_grad):
    sizes = tuple(block.shape[0] for block in blocks)
    places = sum(sizes)
    kind = blocks[0].dtype
    block_shape = blocks[0].shape[1:]
    whole = pl.BlockSpec(memory_space=pltpu.VMEM)
    away = pl.BlockSpec(memory_space=pl.ANY)
    first, last = turn == 0, turn == STAGES - 1
    shape = tile_rows[0].shape
    rows = [distant(x) for x in tile_rows] if first else [held(tile_rows)]
    operands = [sched, *rows, held(stats), *blocks] + ([] if first else [held(query_grad)])
    return pl.pallas_call(
        functools.partial(stage_kernel, turn, sizes),
        out_shape=[
            pltpu.VMEM(shape, kind),
            pltpu.VMEM((places, *block_shape), kind),
            jax.ShapeDtypeStruct((places // 2, *block_shape), kind),
        ] + [pltpu.VMEM((2, *shape), kind)] * first + [jax.ShapeDtypeStruct(shape, kind)] * last,
        in_specs=[pl.BlockSpec(memory_space=pltpu.SMEM)] + ([pl.BlockSpec(memory_space=pltpu.HBM)] * 2 if first else [whole]) + [whole]
        + [away] * len(blocks) + [whole] * (not first),
        out_specs=[whole, whole, away] + [whole] * first + [away] * last,
        scratch_shapes=[
            pltpu.VMEM((places, *block_shape), kind),
            pltpu.SemaphoreType.DMA((len(blocks) + 2,)),
        ],
        input_output_aliases={} if first else {len(operands) - 1: 0},
        compiler_params=pltpu.CompilerParams(vmem_limit_bytes=8 << 20),
        cost_estimate=pl.CostEstimate(
            flops=6 * 10 * 256 * 256 * 128, bytes_accessed=0,
            transcendentals=6 * 65536),
        name=("line_stage", "next_stage", "far_stage")[turn],
    )(*operands)


def add(*parts):
    total = parts[0].astype(jnp.float32)
    for part in parts[1:]:
        total = total + part.astype(jnp.float32)
    return total.astype(jnp.bfloat16)


def shards(queries, output_gradient, prefix_keys, prefix_values, tile_prefix, suffix_lse, suffix_dot):
    tile_count, row_count, _ = queries.shape
    dp = lax.axis_index("dp")
    pos = lax.axis_index("pos")

    own = spread(prefix_keys, prefix_values)
    line = exchange_line(own).reshape(SIDE, 256, 256)
    target = lax.dynamic_slice(tile_prefix, (dp * tile_count, 0), (tile_count, 1)).reshape(1, -1)
    far_z, far_y, far_core = target >> 3, target >> 1 & 3, target & 1
    near = jnp.where(far_core == 0, far_y, far_z)
    far = jnp.where(far_core == 0, (dp >> 3) - far_z, (dp >> 1 & 3) - far_y) & 3
    side = far_core ^ (dp & 1)
    next_one = far & 1
    at = side * (SIDE + SIDE * next_one) + next_one * (far >> 1) * SIDE + near
    code = target * 1024 + jnp.where(far == 0, 0, 2 - next_one) * 256 + at
    code = jnp.pad(code, ((0, 0), (0, 128 - tile_count)))
    sched = plan(code)

    def own_rows(x):
        x = jnp.transpose(x, (0, 2, 1))
        x = lax.dynamic_slice(
            x, (dp * tile_count, 0, pos * row_count), (tile_count, x.shape[1], row_count))
        return x.reshape(tile_count, 1, -1)

    stats = jnp.concatenate([own_rows(suffix_lse), own_rows(suffix_dot)], axis=1)

    line, sched, stats = lax.optimization_barrier((line, sched, stats))
    up, down = shift(line, 1), shift(line, -1)
    here, back = [], []

    def work(turn, block, tile_rows, query_grad):
        query_grad, sums, there, *rest = stage(turn, sched, tile_rows, stats, block, query_grad)
        here.append(sums)
        back.append(swap_cores(there))
        return query_grad, *rest

    def both(*block):
        return [*block, *map(swap_cores, block)]

    query_grad, tile_rows = work(0, both(line), (queries, output_gradient), None)
    up, down, query_grad = lax.optimization_barrier((up, down, query_grad))
    far = shift(up[0:2], 1), shift(down[2:4], -1)
    query_grad, = work(1, both(up, down), tile_rows, query_grad)
    far, query_grad = lax.optimization_barrier((far, query_grad))
    _, query_grad = work(2, both(*far), tile_rows, query_grad)

    from_up = shift(add(here[1][0:4], back[1][0:4]), -1)
    from_down = shift(add(here[1][4:8], back[1][4:8]), 1)
    from_far = shift(add(here[2][0:4], back[2]), 2)
    line_sum = add(here[0][0:4], back[0], from_up, from_down, from_far)
    total = add(*exchange_line(line_sum.reshape(own.shape)))
    return query_grad, total[None, :, 0:128], total[None, :, 128:256]


def solution(mesh):
    in_specs = (
        P("dp", "pos", "head"),
        P("dp", "pos", "head"),
        P("dp", "pos", "head"),
        P("dp", "pos", "head"),
        P(),
        P(None, None, "head"),
        P(None, None, "head"),
    )
    out_specs = (P("dp", "pos", "head"), P("dp", "pos", "head"), P("dp", "pos", "head"))
    return jax.shard_map(shards, mesh=mesh, in_specs=in_specs, out_specs=out_specs, check_vma=False)
```

```python
import functools
import math

import jax
import jax.numpy as jnp
from jax import lax
from jax.experimental import pallas as pl
from jax.experimental.pallas import tpu as pltpu
from jax.sharding import PartitionSpec as P

SIDE = 4
TILES = 24
STAGES = 3
BATCH = 4
LOG2E = math.log2(math.e)
PLACE, TILE, MODE, COUNT, PART = 0, 1, 2, 3, 8


def place(z, y, core):
    return (z % SIDE) * 2 * SIDE + (y % SIDE) * 2 + core


def line_groups():
    groups = []
    for core in range(2):
        for other in range(SIDE):
            ring = [place(other, k, 0) if core == 0 else place(k, other, 1) for k in range(SIDE)]
            groups.append([dp * 2 + pos for dp in ring for pos in range(2)])
    return groups


def exchange_line(x):
    return lax.all_to_all(x, ("dp", "pos"), 0, 0, axis_index_groups=line_groups(), tiled=True)


def shift(x, step):
    pairs = []
    for z in range(SIDE):
        for y in range(SIDE):
            pairs.append((place(z, y, 0), place(z + step, y, 0)))
            pairs.append((place(z, y, 1), place(z, y + step, 1)))
    return lax.ppermute(x, "dp", pairs)


def swap_cores(x):
    return lax.ppermute(x, "dp", [(i, i ^ 1) for i in range(2 * SIDE * SIDE)])


def held(x):
    return pltpu.with_memory_space_constraint(x, pltpu.VMEM)


def distant(x):
    return pltpu.with_memory_space_constraint(x, pltpu.HBM)


def spread_kernel(keys, values, out, both, sem):
    both[:, 0:128] = keys[0]
    both[:, 128:256] = values[0]
    copies = [
        pltpu.make_async_copy(both, out.at[k], sem.at[k]) for k in range(out.shape[0])]
    for copy in copies:
        copy.start()
    for copy in copies:
        copy.wait()


def spread(keys, values):
    whole = pl.BlockSpec(memory_space=pltpu.VMEM)
    return pl.pallas_call(
        spread_kernel,
        out_shape=jax.ShapeDtypeStruct((2 * SIDE, keys.shape[1], 256), keys.dtype),
        in_specs=[whole, whole],
        out_specs=pl.BlockSpec(memory_space=pl.ANY),
        scratch_shapes=[
            pltpu.VMEM((keys.shape[1], 256), keys.dtype),
            pltpu.SemaphoreType.DMA((2 * SIDE,)),
        ],
        name="spread",
    )(keys, values)


def settle_kernel(source, target, sem):
    copy = pltpu.make_async_copy(source, target, sem)
    copy.start()
    copy.wait()


def settle(x):
    return pl.pallas_call(
        settle_kernel,
        out_shape=jax.ShapeDtypeStruct(x.shape, x.dtype),
        in_specs=[pl.BlockSpec(memory_space=pltpu.VMEM)],
        out_specs=pl.BlockSpec(memory_space=pl.ANY),
        scratch_shapes=[pltpu.SemaphoreType.DMA],
        compiler_params=pltpu.CompilerParams(vmem_limit_bytes=1 << 20),
        name="settle",
    )(held(x))


def plan_kernel(code_ref, out):
    shape = (TILES, 128)
    lane = lax.broadcasted_iota(jnp.int32, shape, 1)
    row = lax.broadcasted_iota(jnp.int32, shape, 0)
    code = jnp.broadcast_to(code_ref[...], shape)
    mine = jnp.sum(jnp.where(lane == row, code, 0), axis=1, keepdims=True)
    code = jnp.where(lane < TILES, code, -1)
    twin = (code >> 10 == mine >> 10) & (lane != row)
    dup = jnp.sum(twin.astype(jnp.int32), axis=1, keepdims=True)
    stage = mine >> 8 & 3
    at = mine & 255
    key = stage * 4096 + (1 - dup) * 2048 + at * 32 + row[:, 0:1]
    keys = jnp.sum(jnp.where(lane == row, key, 0), axis=0, keepdims=True)
    ahead = (keys < key) & (keys >> 12 == stage) & (lane < TILES)
    rank = jnp.sum(ahead.astype(jnp.int32), axis=1, keepdims=True)
    for turn in range(STAGES):
        here = stage == turn
        n = jnp.sum(jnp.where(here & (lane == 0), 1, 0))
        last = jnp.maximum((n + 1) // 2 - 1, 0)
        pair = jnp.minimum(lane // 2, last)
        source = jnp.maximum(jnp.minimum(2 * pair + lane % 2, n - 1), 0)
        picked = here & (rank == source)
        first = PART * turn

        def put(line, value, chosen):
            out[first + line:first + line + 1, :] = jnp.sum(
                jnp.where(chosen, value, 0), axis=0, keepdims=True)

        put(PLACE, at, picked)
        put(TILE, row, picked)
        put(MODE, dup, picked)
        out[first + COUNT:first + COUNT + 1, :] = jnp.full((1, 128), (n + BATCH - 1) // BATCH)


def plan(code):
    whole = pl.BlockSpec(memory_space=pltpu.VMEM)
    return pl.pallas_call(
        plan_kernel,
        out_shape=pltpu.VMEM((STAGES * PART, 128), jnp.int32),
        in_specs=[whole],
        out_specs=whole,
        name="plan",
    )(code)


def tile_grads(query, grad, keys, values, stat, scaling):
    nt = (((1,), (1,)), ((), ()))
    tn = (((0,), (0,)), ((), ()))
    f32, half = jnp.float32, jnp.bfloat16
    tiles = range(len(query))
    scores = [
        lax.dot_general(keys[k], query[k], nt, preferred_element_type=f32) * (scaling * LOG2E)
        for k in tiles
    ]
    prob_grad = [
        lax.dot_general(values[k], grad[k], nt, preferred_element_type=f32) for k in tiles
    ]
    prob_half, score_grad = [], []
    for k in tiles:
        suffix_l = stat[k][0:1] * LOG2E
        suffix_d = stat[k][1:2]
        top = jnp.maximum(jnp.max(scores[k], axis=0, keepdims=True), suffix_l)
        raised = jnp.exp2(scores[k] - top)
        suffix_part = jnp.exp2(suffix_l - top)
        inverse = 1.0 / (jnp.sum(raised, axis=0, keepdims=True) + suffix_part)
        moment = jnp.sum(raised * prob_grad[k], axis=0, keepdims=True) + suffix_part * suffix_d
        probs = raised * inverse
        prob_half.append(probs.astype(half))
        score_grad.append((probs * (prob_grad[k] - moment * inverse)).astype(half))
    parts = []
    for k in tiles:
        query_part = lax.dot_general(keys[k], score_grad[k], tn, preferred_element_type=f32)
        parts.append((
            (query_part * scaling).astype(half).T,
            jnp.dot(score_grad[k], query[k], preferred_element_type=f32) * scaling,
            jnp.dot(prob_half[k], grad[k], preferred_element_type=f32),
        ))
    return parts


def stage_kernel(turn, sizes, sched, *refs):
    if turn == 0:
        queries, grads, stats, *blocks = refs[:3 + len(sizes)]
        query_grad, sums, there, tile_rows, near, arrived = refs[3 + len(sizes):]
    else:
        tile_rows, stats, *blocks = refs[:2 + len(sizes)]
        query_grad, sums, there, near, arrived = refs[3 + len(sizes):]
    _, _, rows, width = tile_rows.shape
    heads = width // 128
    scaling = 128 ** -0.5
    base = turn * PART
    places = sums.shape[0]
    count = sched[base + COUNT, 0]
    loads, first = [], 0
    for block, size in zip(blocks, sizes):
        loads.append(pltpu.make_async_copy(
            block, near.at[first:first + size], arrived.at[len(loads)]))
        first += size
    if turn == 0:
        for which, source in enumerate((queries, grads)):
            loads.append(pltpu.make_async_copy(
                source, tile_rows.at[which], arrived.at[len(loads)]))
    for load in loads:
        load.start()
    sums[...] = jnp.zeros(sums.shape, sums.dtype)
    for load in loads:
        load.wait()

    def stacked(which, tile):
        return jnp.concatenate(
            [tile_rows[which, tile, :, h * 128:(h + 1) * 128] for h in range(heads)], axis=0)

    def step(batch, _):
        at = [sched[base + PLACE, batch * BATCH + k] for k in range(BATCH)]
        tile = [sched[base + TILE, batch * BATCH + k] for k in range(BATCH)]
        twins = [sched[base + MODE, batch * BATCH + 2 * pair] for pair in range(BATCH // 2)]
        parts = tile_grads(
            [stacked(0, t) for t in tile], [stacked(1, t) for t in tile],
            [near[k, :, 0:128] for k in at], [near[k, :, 128:256] for k in at],
            [stats[t] for t in tile], scaling)
        for k in range(BATCH):
            for h in range(heads):
                query_grad[tile[k], :, h * 128:(h + 1) * 128] = parts[k][0][h * rows:(h + 1) * rows]
        for pair in range(BATCH // 2):
            a, b = 2 * pair, 2 * pair + 1
            other = jnp.where(twins[pair] == 1, 1.0, 0.0)
            for one, two in ((a, b), (b, a)):
                for part in (1, 2):
                    sums[at[one], :, part * 128 - 128:part * 128] = (
                        parts[one][part] + other * parts[two][part]).astype(sums.dtype)
        return 0

    lax.fori_loop(0, count, step, 0)
    handed = pltpu.make_async_copy(sums.at[places // 2:places], there, arrived.at[0])
    handed.start()
    handed.wait()


def stage(turn, sched, tile_rows, stats, blocks, query_grad):
    sizes = tuple(block.shape[0] for block in blocks)
    places = sum(sizes)
    kind = blocks[0].dtype
    block_shape = blocks[0].shape[1:]
    whole = pl.BlockSpec(memory_space=pltpu.VMEM)
    away = pl.BlockSpec(memory_space=pl.ANY)
    first = turn == 0
    shape = tile_rows[0].shape
    rows = [distant(x) for x in tile_rows] if first else [held(tile_rows)]
    operands = [sched, *rows, held(stats), *blocks] + ([] if first else [held(query_grad)])
    return pl.pallas_call(
        functools.partial(stage_kernel, turn, sizes),
        out_shape=[
            pltpu.VMEM(shape, kind),
            pltpu.VMEM((places, *block_shape), kind),
            jax.ShapeDtypeStruct((places // 2, *block_shape), kind),
        ] + [pltpu.VMEM((2, *shape), kind)] * first,
        in_specs=[pl.BlockSpec(memory_space=pltpu.SMEM)] + ([pl.BlockSpec(memory_space=pltpu.HBM)] * 2 if first else [whole]) + [whole]
        + [away] * len(blocks) + [whole] * (not first),
        out_specs=[whole, whole, away] + [whole] * first,
        scratch_shapes=[
            pltpu.VMEM((places, *block_shape), kind),
            pltpu.SemaphoreType.DMA((len(blocks) + 2,)),
        ],
        input_output_aliases={} if first else {len(operands) - 1: 0},
        compiler_params=pltpu.CompilerParams(vmem_limit_bytes=8 << 20),
        cost_estimate=pl.CostEstimate(
            flops=6 * 10 * 256 * 256 * 128, bytes_accessed=0,
            transcendentals=6 * 65536),
        name=("line_stage", "next_stage", "far_stage")[turn],
    )(*operands)


def wide(*parts):
    total = parts[0].astype(jnp.float32)
    for part in parts[1:]:
        total = total + part.astype(jnp.float32)
    return total


def add(*parts):
    return wide(*parts).astype(jnp.bfloat16)


def shards(queries, output_gradient, prefix_keys, prefix_values, tile_prefix, suffix_lse, suffix_dot):
    tile_count, row_count, _ = queries.shape
    dp = lax.axis_index("dp")
    pos = lax.axis_index("pos")

    own = spread(prefix_keys, prefix_values)
    line = exchange_line(own).reshape(SIDE, 256, 256)
    target = lax.dynamic_slice(tile_prefix, (dp * tile_count, 0), (tile_count, 1)).reshape(1, -1)
    far_z, far_y, far_core = target >> 3, target >> 1 & 3, target & 1
    near = jnp.where(far_core == 0, far_y, far_z)
    far = jnp.where(far_core == 0, (dp >> 3) - far_z, (dp >> 1 & 3) - far_y) & 3
    side = far_core ^ (dp & 1)
    next_one = far & 1
    at = side * (SIDE + SIDE * next_one) + next_one * (far >> 1) * SIDE + near
    code = target * 1024 + jnp.where(far == 0, 0, 2 - next_one) * 256 + at
    code = jnp.pad(code, ((0, 0), (0, 128 - tile_count)))
    sched = plan(code)

    def own_rows(x):
        x = jnp.transpose(x, (0, 2, 1))
        x = lax.dynamic_slice(
            x, (dp * tile_count, 0, pos * row_count), (tile_count, x.shape[1], row_count))
        return x.reshape(tile_count, 1, -1)

    stats = jnp.concatenate([own_rows(suffix_lse), own_rows(suffix_dot)], axis=1)

    line, sched, stats = lax.optimization_barrier((line, sched, stats))
    up, down = shift(line, 1), shift(line, -1)
    here, back = [], []

    def work(turn, block, tile_rows, query_grad):
        query_grad, sums, there, *rest = stage(turn, sched, tile_rows, stats, block, query_grad)
        here.append(sums)
        back.append(there)
        return query_grad, *rest

    def both(*block):
        return [*block, *map(swap_cores, block)]

    query_grad, tile_rows = work(0, both(line), (queries, output_gradient), None)
    up, down, query_grad = lax.optimization_barrier((up, down, query_grad))
    far = shift(up[0:2], 1), shift(down[2:4], -1)
    query_grad, = work(1, both(up, down), tile_rows, query_grad)
    far, query_grad = lax.optimization_barrier((far, query_grad))
    others = [swap_cores(x) for x in far]
    back[1], *others = lax.optimization_barrier((back[1], *others))
    query_grad, = work(2, [*far, *others], tile_rows, query_grad)
    back = [swap_cores(x) for x in back]

    to_up, to_down = add(here[1][0:4], back[1][0:4]), add(here[1][4:8], back[1][4:8])
    to_up, to_down, back[2] = lax.optimization_barrier((to_up, to_down, back[2]))
    from_up, from_down = shift(to_up, -1), shift(to_down, 1)
    from_far = shift(add(here[2][0:4], back[2]), 2)
    query_grad = settle(query_grad)
    near_sum, query_grad = lax.optimization_barrier(
        (wide(here[0][0:4], back[0], from_up, from_down), query_grad))
    line_sum = add(near_sum, from_far)
    total = add(*exchange_line(line_sum.reshape(own.shape)))
    return query_grad, total[None, :, 0:128], total[None, :, 128:256]


def solution(mesh):
    in_specs = (
        P("dp", "pos", "head"),
        P("dp", "pos", "head"),
        P("dp", "pos", "head"),
        P("dp", "pos", "head"),
        P(),
        P(None, None, "head"),
        P(None, None, "head"),
    )
    out_specs = (P("dp", "pos", "head"), P("dp", "pos", "head"), P("dp", "pos", "head"))
    return jax.shard_map(shards, mesh=mesh, in_specs=in_specs, out_specs=out_specs, check_vma=False)
```

```python
import functools
import math

import jax
import jax.numpy as jnp
from jax import lax
from jax.experimental import pallas as pl
from jax.experimental.pallas import tpu as pltpu
from jax.sharding import PartitionSpec as P

SIDE = 4
TILES = 24
STAGES = 3
BATCH = 4
LOG2E = math.log2(math.e)
PLACE, TILE, MODE, COUNT, PART = 0, 1, 2, 3, 8


def place(z, y, core):
    return (z % SIDE) * 2 * SIDE + (y % SIDE) * 2 + core


def line_groups():
    groups = []
    for core in range(2):
        for other in range(SIDE):
            ring = [place(other, k, 0) if core == 0 else place(k, other, 1) for k in range(SIDE)]
            groups.append([dp * 2 + pos for dp in ring for pos in range(2)])
    return groups


def exchange_line(x):
    return lax.all_to_all(x, ("dp", "pos"), 0, 0, axis_index_groups=line_groups(), tiled=True)


def shift(x, step):
    pairs = []
    for z in range(SIDE):
        for y in range(SIDE):
            pairs.append((place(z, y, 0), place(z + step, y, 0)))
            pairs.append((place(z, y, 1), place(z, y + step, 1)))
    return lax.ppermute(x, "dp", pairs)


def swap_cores(x):
    return lax.ppermute(x, "dp", [(i, i ^ 1) for i in range(2 * SIDE * SIDE)])


def held(x):
    return pltpu.with_memory_space_constraint(x, pltpu.VMEM)


def distant(x):
    return pltpu.with_memory_space_constraint(x, pltpu.HBM)


def spread_kernel(keys, values, out, both, sem):
    both[:, 0:128] = keys[0]
    both[:, 128:256] = values[0]
    copies = [
        pltpu.make_async_copy(both, out.at[k], sem.at[k]) for k in range(out.shape[0])]
    for copy in copies:
        copy.start()
    for copy in copies:
        copy.wait()


def spread(keys, values):
    whole = pl.BlockSpec(memory_space=pltpu.VMEM)
    return pl.pallas_call(
        spread_kernel,
        out_shape=jax.ShapeDtypeStruct((2 * SIDE, keys.shape[1], 256), keys.dtype),
        in_specs=[whole, whole],
        out_specs=pl.BlockSpec(memory_space=pl.ANY),
        scratch_shapes=[
            pltpu.VMEM((keys.shape[1], 256), keys.dtype),
            pltpu.SemaphoreType.DMA((2 * SIDE,)),
        ],
        name="spread",
    )(keys, values)


def settle_kernel(source, target, sem):
    copy = pltpu.make_async_copy(source, target, sem)
    copy.start()
    copy.wait()


def settle(x):
    return pl.pallas_call(
        settle_kernel,
        out_shape=jax.ShapeDtypeStruct(x.shape, x.dtype),
        in_specs=[pl.BlockSpec(memory_space=pltpu.VMEM)],
        out_specs=pl.BlockSpec(memory_space=pl.ANY),
        scratch_shapes=[pltpu.SemaphoreType.DMA],
        compiler_params=pltpu.CompilerParams(vmem_limit_bytes=1 << 20),
        name="settle",
    )(held(x))


def plan_kernel(code_ref, out):
    shape = (TILES, 128)
    lane = lax.broadcasted_iota(jnp.int32, shape, 1)
    row = lax.broadcasted_iota(jnp.int32, shape, 0)
    code = jnp.broadcast_to(code_ref[...], shape)
    mine = jnp.sum(jnp.where(lane == row, code, 0), axis=1, keepdims=True)
    code = jnp.where(lane < TILES, code, -1)
    twin = (code >> 10 == mine >> 10) & (lane != row)
    dup = jnp.sum(twin.astype(jnp.int32), axis=1, keepdims=True)
    stage = mine >> 8 & 3
    at = mine & 255
    key = stage * 4096 + (1 - dup) * 2048 + at * 32 + row[:, 0:1]
    keys = jnp.sum(jnp.where(lane == row, key, 0), axis=0, keepdims=True)
    ahead = (keys < key) & (keys >> 12 == stage) & (lane < TILES)
    rank = jnp.sum(ahead.astype(jnp.int32), axis=1, keepdims=True)
    for turn in range(STAGES):
        here = stage == turn
        n = jnp.sum(jnp.where(here & (lane == 0), 1, 0))
        last = jnp.maximum((n + 1) // 2 - 1, 0)
        pair = jnp.minimum(lane // 2, last)
        source = jnp.maximum(jnp.minimum(2 * pair + lane % 2, n - 1), 0)
        picked = here & (rank == source)
        first = PART * turn

        def put(line, value, chosen):
            out[first + line:first + line + 1, :] = jnp.sum(
                jnp.where(chosen, value, 0), axis=0, keepdims=True)

        put(PLACE, at, picked)
        put(TILE, row, picked)
        put(MODE, dup, picked)
        out[first + COUNT:first + COUNT + 1, :] = jnp.full((1, 128), (n + BATCH - 1) // BATCH)


def plan(code):
    whole = pl.BlockSpec(memory_space=pltpu.VMEM)
    return pl.pallas_call(
        plan_kernel,
        out_shape=pltpu.VMEM((STAGES * PART, 128), jnp.int32),
        in_specs=[whole],
        out_specs=whole,
        name="plan",
    )(code)


def tile_grads(query, grad, keys, values, stat, scaling):
    nt = (((1,), (1,)), ((), ()))
    tn = (((0,), (0,)), ((), ()))
    f32, half = jnp.float32, jnp.bfloat16
    tiles = range(len(query))
    scores = [
        lax.dot_general(keys[k], query[k], nt, preferred_element_type=f32) * (scaling * LOG2E)
        for k in tiles
    ]
    prob_grad = [
        lax.dot_general(values[k], grad[k], nt, preferred_element_type=f32) for k in tiles
    ]
    prob_half, score_grad = [], []
    for k in tiles:
        suffix_l = stat[k][0:1] * LOG2E
        suffix_d = stat[k][1:2]
        top = jnp.maximum(jnp.max(scores[k], axis=0, keepdims=True), suffix_l)
        raised = jnp.exp2(scores[k] - top)
        suffix_part = jnp.exp2(suffix_l - top)
        inverse = 1.0 / (jnp.sum(raised, axis=0, keepdims=True) + suffix_part)
        moment = jnp.sum(raised * prob_grad[k], axis=0, keepdims=True) + suffix_part * suffix_d
        probs = raised * inverse
        prob_half.append(probs.astype(half))
        score_grad.append((probs * (prob_grad[k] - moment * inverse)).astype(half))
    parts = []
    for k in tiles:
        query_part = lax.dot_general(keys[k], score_grad[k], tn, preferred_element_type=f32)
        parts.append((
            (query_part * scaling).astype(half).T,
            jnp.dot(score_grad[k], query[k], preferred_element_type=f32) * scaling,
            jnp.dot(prob_half[k], grad[k], preferred_element_type=f32),
        ))
    return parts


def stage_kernel(turn, sizes, sched, *refs):
    if turn == 0:
        queries, grads, stats, *blocks = refs[:3 + len(sizes)]
        query_grad, sums, there, tile_rows, near, arrived = refs[3 + len(sizes):]
    else:
        tile_rows, stats, *blocks = refs[:2 + len(sizes)]
        query_grad, sums, there, near, arrived = refs[3 + len(sizes):]
    _, _, rows, width = tile_rows.shape
    heads = width // 128
    scaling = 128 ** -0.5
    base = turn * PART
    places = sums.shape[0]
    count = sched[base + COUNT, 0]
    loads, first = [], 0
    for block, size in zip(blocks, sizes):
        loads.append(pltpu.make_async_copy(
            block, near.at[first:first + size], arrived.at[len(loads)]))
        first += size
    if turn == 0:
        for which, source in enumerate((queries, grads)):
            loads.append(pltpu.make_async_copy(
                source, tile_rows.at[which], arrived.at[len(loads)]))
    for load in loads:
        load.start()
    sums[...] = jnp.zeros(sums.shape, sums.dtype)
    for load in loads:
        load.wait()

    def stacked(which, tile):
        return jnp.concatenate(
            [tile_rows[which, tile, :, h * 128:(h + 1) * 128] for h in range(heads)], axis=0)

    def step(batch, _):
        at = [sched[base + PLACE, batch * BATCH + k] for k in range(BATCH)]
        tile = [sched[base + TILE, batch * BATCH + k] for k in range(BATCH)]
        twins = [sched[base + MODE, batch * BATCH + 2 * pair] for pair in range(BATCH // 2)]
        parts = tile_grads(
            [stacked(0, t) for t in tile], [stacked(1, t) for t in tile],
            [near[k, :, 0:128] for k in at], [near[k, :, 128:256] for k in at],
            [stats[t] for t in tile], scaling)
        for k in range(BATCH):
            for h in range(heads):
                query_grad[tile[k], :, h * 128:(h + 1) * 128] = parts[k][0][h * rows:(h + 1) * rows]
        for pair in range(BATCH // 2):
            a, b = 2 * pair, 2 * pair + 1
            other = jnp.where(twins[pair] == 1, 1.0, 0.0)
            for one, two in ((a, b), (b, a)):
                for part in (1, 2):
                    sums[at[one], :, part * 128 - 128:part * 128] = (
                        parts[one][part] + other * parts[two][part]).astype(sums.dtype)
        return 0

    lax.fori_loop(0, count, step, 0)
    handed = pltpu.make_async_copy(sums.at[places // 2:places], there, arrived.at[0])
    handed.start()
    handed.wait()


def stage(turn, sched, tile_rows, stats, blocks, query_grad):
    sizes = tuple(block.shape[0] for block in blocks)
    places = sum(sizes)
    kind = blocks[0].dtype
    block_shape = blocks[0].shape[1:]
    whole = pl.BlockSpec(memory_space=pltpu.VMEM)
    away = pl.BlockSpec(memory_space=pl.ANY)
    first = turn == 0
    shape = tile_rows[0].shape
    rows = [distant(x) for x in tile_rows] if first else [held(tile_rows)]
    operands = [sched, *rows, held(stats), *blocks] + ([] if first else [held(query_grad)])
    return pl.pallas_call(
        functools.partial(stage_kernel, turn, sizes),
        out_shape=[
            pltpu.VMEM(shape, kind),
            pltpu.VMEM((places, *block_shape), kind),
            jax.ShapeDtypeStruct((places // 2, *block_shape), kind),
        ] + [pltpu.VMEM((2, *shape), kind)] * first,
        in_specs=[pl.BlockSpec(memory_space=pltpu.SMEM)] + ([pl.BlockSpec(memory_space=pltpu.HBM)] * 2 if first else [whole]) + [whole]
        + [away] * len(blocks) + [whole] * (not first),
        out_specs=[whole, whole, away] + [whole] * first,
        scratch_shapes=[
            pltpu.VMEM((places, *block_shape), kind),
            pltpu.SemaphoreType.DMA((len(blocks) + 2,)),
        ],
        input_output_aliases={} if first else {len(operands) - 1: 0},
        compiler_params=pltpu.CompilerParams(vmem_limit_bytes=8 << 20),
        cost_estimate=pl.CostEstimate(
            flops=6 * 10 * 256 * 256 * 128, bytes_accessed=0,
            transcendentals=6 * 65536),
        name=("line_stage", "next_stage", "far_stage")[turn],
    )(*operands)


def wide(*parts):
    total = parts[0].astype(jnp.float32)
    for part in parts[1:]:
        total = total + part.astype(jnp.float32)
    return total


def add(*parts):
    return wide(*parts).astype(jnp.bfloat16)


def shards(queries, output_gradient, prefix_keys, prefix_values, tile_prefix, suffix_lse, suffix_dot):
    tile_count, row_count, _ = queries.shape
    dp = lax.axis_index("dp")
    pos = lax.axis_index("pos")

    own = spread(prefix_keys, prefix_values)
    line = exchange_line(own).reshape(SIDE, 256, 256)
    target = lax.dynamic_slice(tile_prefix, (dp * tile_count, 0), (tile_count, 1)).reshape(1, -1)
    far_z, far_y, far_core = target >> 3, target >> 1 & 3, target & 1
    near = jnp.where(far_core == 0, far_y, far_z)
    far = jnp.where(far_core == 0, (dp >> 3) - far_z, (dp >> 1 & 3) - far_y) & 3
    side = far_core ^ (dp & 1)
    next_one = far & 1
    at = side * (SIDE + SIDE * next_one) + next_one * (far >> 1) * SIDE + near
    code = target * 1024 + jnp.where(far == 0, 0, 2 - next_one) * 256 + at
    code = jnp.pad(code, ((0, 0), (0, 128 - tile_count)))
    sched = plan(code)

    def own_rows(x):
        x = jnp.transpose(x, (0, 2, 1))
        x = lax.dynamic_slice(
            x, (dp * tile_count, 0, pos * row_count), (tile_count, x.shape[1], row_count))
        return x.reshape(tile_count, 1, -1)

    stats = jnp.concatenate([own_rows(suffix_lse), own_rows(suffix_dot)], axis=1)

    line, sched, stats = lax.optimization_barrier((line, sched, stats))
    up, down = shift(line, 1), shift(line, -1)
    here, back = [], []

    def work(turn, block, tile_rows, query_grad):
        query_grad, sums, there, *rest = stage(turn, sched, tile_rows, stats, block, query_grad)
        here.append(sums)
        back.append(there)
        return query_grad, *rest

    def both(*block):
        return [*block, *map(swap_cores, block)]

    query_grad, tile_rows = work(0, both(line), (queries, output_gradient), None)
    up, down, query_grad = lax.optimization_barrier((up, down, query_grad))
    far = shift(up[0:2], 1), shift(down[2:4], -1)
    query_grad, = work(1, both(up, down), tile_rows, query_grad)
    far, query_grad = lax.optimization_barrier((far, query_grad))
    others = [swap_cores(x) for x in far]
    back[1], *others = lax.optimization_barrier((back[1], *others))
    query_grad, = work(2, [*far, *others], tile_rows, query_grad)
    back = [swap_cores(x) for x in back]

    to_up, to_down = add(here[1][0:4], back[1][0:4]), add(here[1][4:8], back[1][4:8])
    _, _, back[2] = lax.optimization_barrier((to_up, to_down, back[2]))
    from_up, from_down = shift(to_up, -1), shift(to_down, 1)
    from_far = shift(add(here[2][0:4], back[2]), 2)
    query_grad = settle(query_grad)
    near_sum, query_grad = lax.optimization_barrier(
        (wide(here[0][0:4], back[0], from_up, from_down), query_grad))
    line_sum = add(near_sum, from_far)
    total = add(*exchange_line(line_sum.reshape(own.shape)))
    return query_grad, total[None, :, 0:128], total[None, :, 128:256]


def solution(mesh):
    in_specs = (
        P("dp", "pos", "head"),
        P("dp", "pos", "head"),
        P("dp", "pos", "head"),
        P("dp", "pos", "head"),
        P(),
        P(None, None, "head"),
        P(None, None, "head"),
    )
    out_specs = (P("dp", "pos", "head"), P("dp", "pos", "head"), P("dp", "pos", "head"))
    return jax.shard_map(shards, mesh=mesh, in_specs=in_specs, out_specs=out_specs, check_vma=False)
```

```python
import functools
import math

import jax
import jax.numpy as jnp
from jax import lax
from jax.experimental import pallas as pl
from jax.experimental.pallas import tpu as pltpu
from jax.sharding import PartitionSpec as P

SIDE = 4
TILES = 24
STAGES = 3
BATCH = 4
LOG2E = math.log2(math.e)
PLACE, TILE, MODE, COUNT, PART = 0, 1, 2, 3, 8


def place(z, y, core):
    return (z % SIDE) * 2 * SIDE + (y % SIDE) * 2 + core


def line_groups():
    groups = []
    for core in range(2):
        for other in range(SIDE):
            ring = [place(other, k, 0) if core == 0 else place(k, other, 1) for k in range(SIDE)]
            groups.append([dp * 2 + pos for dp in ring for pos in range(2)])
    return groups


def exchange_line(x):
    return lax.all_to_all(x, ("dp", "pos"), 0, 0, axis_index_groups=line_groups(), tiled=True)


def shift(x, step):
    pairs = []
    for z in range(SIDE):
        for y in range(SIDE):
            pairs.append((place(z, y, 0), place(z + step, y, 0)))
            pairs.append((place(z, y, 1), place(z, y + step, 1)))
    return lax.ppermute(x, "dp", pairs)


def swap_cores(x):
    return lax.ppermute(x, "dp", [(i, i ^ 1) for i in range(2 * SIDE * SIDE)])


def held(x):
    return pltpu.with_memory_space_constraint(x, pltpu.VMEM)


def distant(x):
    return pltpu.with_memory_space_constraint(x, pltpu.HBM)


def spread_kernel(keys, values, out, both, sem):
    both[:, 0:128] = keys[0]
    both[:, 128:256] = values[0]
    copies = [
        pltpu.make_async_copy(both, out.at[k], sem.at[k]) for k in range(out.shape[0])]
    for copy in copies:
        copy.start()
    for copy in copies:
        copy.wait()


def spread(keys, values):
    whole = pl.BlockSpec(memory_space=pltpu.VMEM)
    return pl.pallas_call(
        spread_kernel,
        out_shape=jax.ShapeDtypeStruct((2 * SIDE, keys.shape[1], 256), keys.dtype),
        in_specs=[whole, whole],
        out_specs=pl.BlockSpec(memory_space=pl.ANY),
        scratch_shapes=[
            pltpu.VMEM((keys.shape[1], 256), keys.dtype),
            pltpu.SemaphoreType.DMA((2 * SIDE,)),
        ],
        name="spread",
    )(keys, values)


def settle_kernel(source, target, sem):
    copy = pltpu.make_async_copy(source, target, sem)
    copy.start()
    copy.wait()


def settle(x):
    return pl.pallas_call(
        settle_kernel,
        out_shape=jax.ShapeDtypeStruct(x.shape, x.dtype),
        in_specs=[pl.BlockSpec(memory_space=pltpu.VMEM)],
        out_specs=pl.BlockSpec(memory_space=pl.ANY),
        scratch_shapes=[pltpu.SemaphoreType.DMA],
        compiler_params=pltpu.CompilerParams(vmem_limit_bytes=1 << 20),
        name="settle",
    )(held(x))


def plan_kernel(code_ref, out):
    shape = (TILES, 128)
    lane = lax.broadcasted_iota(jnp.int32, shape, 1)
    row = lax.broadcasted_iota(jnp.int32, shape, 0)
    code = jnp.broadcast_to(code_ref[...], shape)
    mine = jnp.sum(jnp.where(lane == row, code, 0), axis=1, keepdims=True)
    code = jnp.where(lane < TILES, code, -1)
    twin = (code >> 10 == mine >> 10) & (lane != row)
    dup = jnp.sum(twin.astype(jnp.int32), axis=1, keepdims=True)
    stage = mine >> 8 & 3
    at = mine & 255
    key = stage * 4096 + (1 - dup) * 2048 + at * 32 + row[:, 0:1]
    keys = jnp.sum(jnp.where(lane == row, key, 0), axis=0, keepdims=True)
    ahead = (keys < key) & (keys >> 12 == stage) & (lane < TILES)
    rank = jnp.sum(ahead.astype(jnp.int32), axis=1, keepdims=True)
    for turn in range(STAGES):
        here = stage == turn
        n = jnp.sum(jnp.where(here & (lane == 0), 1, 0))
        last = jnp.maximum((n + 1) // 2 - 1, 0)
        pair = jnp.minimum(lane // 2, last)
        source = jnp.maximum(jnp.minimum(2 * pair + lane % 2, n - 1), 0)
        picked = here & (rank == source)
        first = PART * turn

        def put(line, value, chosen):
            out[first + line:first + line + 1, :] = jnp.sum(
                jnp.where(chosen, value, 0), axis=0, keepdims=True)

        put(PLACE, at, picked)
        put(TILE, row, picked)
        put(MODE, dup, picked)
        out[first + COUNT:first + COUNT + 1, :] = jnp.full((1, 128), (n + BATCH - 1) // BATCH)


def plan(code):
    whole = pl.BlockSpec(memory_space=pltpu.VMEM)
    return pl.pallas_call(
        plan_kernel,
        out_shape=pltpu.VMEM((STAGES * PART, 128), jnp.int32),
        in_specs=[whole],
        out_specs=whole,
        name="plan",
    )(code)


def tile_grads(query, grad, keys, values, stat, scaling):
    nt = (((1,), (1,)), ((), ()))
    tn = (((0,), (0,)), ((), ()))
    f32, half = jnp.float32, jnp.bfloat16
    tiles = range(len(query))
    scores = [
        lax.dot_general(keys[k], query[k], nt, preferred_element_type=f32) * (scaling * LOG2E)
        for k in tiles
    ]
    prob_grad = [
        lax.dot_general(values[k], grad[k], nt, preferred_element_type=f32) for k in tiles
    ]
    prob_half, score_grad = [], []
    for k in tiles:
        suffix_l = stat[k][0:1] * LOG2E
        suffix_d = stat[k][1:2]
        top = jnp.maximum(jnp.max(scores[k], axis=0, keepdims=True), suffix_l)
        raised = jnp.exp2(scores[k] - top)
        suffix_part = jnp.exp2(suffix_l - top)
        inverse = 1.0 / (jnp.sum(raised, axis=0, keepdims=True) + suffix_part)
        moment = jnp.sum(raised * prob_grad[k], axis=0, keepdims=True) + suffix_part * suffix_d
        probs = raised * inverse
        prob_half.append(probs.astype(half))
        score_grad.append((probs * (prob_grad[k] - moment * inverse)).astype(half))
    parts = []
    for k in tiles:
        query_part = lax.dot_general(keys[k], score_grad[k], tn, preferred_element_type=f32)
        parts.append((
            (query_part * scaling).astype(half).T,
            jnp.dot(score_grad[k], query[k], preferred_element_type=f32) * scaling,
            jnp.dot(prob_half[k], grad[k], preferred_element_type=f32),
        ))
    return parts


def stage_kernel(turn, sizes, sched, *refs):
    if turn == 0:
        queries, grads, stats, *blocks = refs[:3 + len(sizes)]
        query_grad, sums, there, tile_rows, near, arrived = refs[3 + len(sizes):]
    else:
        tile_rows, stats, *blocks = refs[:2 + len(sizes)]
        query_grad, sums, there, near, arrived = refs[3 + len(sizes):]
    _, _, rows, width = tile_rows.shape
    heads = width // 128
    scaling = 128 ** -0.5
    base = turn * PART
    places = sums.shape[0]
    count = sched[base + COUNT, 0]
    loads, first = [], 0
    for block, size in zip(blocks, sizes):
        loads.append(pltpu.make_async_copy(
            block, near.at[first:first + size], arrived.at[len(loads)]))
        first += size
    if turn == 0:
        for which, source in enumerate((queries, grads)):
            loads.append(pltpu.make_async_copy(
                source, tile_rows.at[which], arrived.at[len(loads)]))
    for load in loads:
        load.start()
    sums[...] = jnp.zeros(sums.shape, sums.dtype)
    for load in loads:
        load.wait()

    def stacked(which, tile):
        return jnp.concatenate(
            [tile_rows[which, tile, :, h * 128:(h + 1) * 128] for h in range(heads)], axis=0)

    def step(batch, _):
        at = [sched[base + PLACE, batch * BATCH + k] for k in range(BATCH)]
        tile = [sched[base + TILE, batch * BATCH + k] for k in range(BATCH)]
        twins = [sched[base + MODE, batch * BATCH + 2 * pair] for pair in range(BATCH // 2)]
        parts = tile_grads(
            [stacked(0, t) for t in tile], [stacked(1, t) for t in tile],
            [near[k, :, 0:128] for k in at], [near[k, :, 128:256] for k in at],
            [stats[t] for t in tile], scaling)
        for k in range(BATCH):
            for h in range(heads):
                query_grad[tile[k], :, h * 128:(h + 1) * 128] = parts[k][0][h * rows:(h + 1) * rows]
        for pair in range(BATCH // 2):
            a, b = 2 * pair, 2 * pair + 1
            other = jnp.where(twins[pair] == 1, 1.0, 0.0)
            for one, two in ((a, b), (b, a)):
                for part in (1, 2):
                    sums[at[one], :, part * 128 - 128:part * 128] = (
                        parts[one][part] + other * parts[two][part]).astype(sums.dtype)
        return 0

    lax.fori_loop(0, count, step, 0)
    there[...] = sums[places // 2:places]


def stage(turn, sched, tile_rows, stats, blocks, query_grad):
    sizes = tuple(block.shape[0] for block in blocks)
    places = sum(sizes)
    kind = blocks[0].dtype
    block_shape = blocks[0].shape[1:]
    whole = pl.BlockSpec(memory_space=pltpu.VMEM)
    away = pl.BlockSpec(memory_space=pl.ANY)
    first = turn == 0
    shape = tile_rows[0].shape
    rows = [distant(x) for x in tile_rows] if first else [held(tile_rows)]
    operands = [sched, *rows, held(stats), *blocks] + ([] if first else [held(query_grad)])
    return pl.pallas_call(
        functools.partial(stage_kernel, turn, sizes),
        out_shape=[
            pltpu.VMEM(shape, kind),
            pltpu.VMEM((places, *block_shape), kind),
            pltpu.VMEM((places // 2, *block_shape), kind),
        ] + [pltpu.VMEM((2, *shape), kind)] * first,
        in_specs=[pl.BlockSpec(memory_space=pltpu.SMEM)] + ([pl.BlockSpec(memory_space=pltpu.HBM)] * 2 if first else [whole]) + [whole]
        + [away] * len(blocks) + [whole] * (not first),
        out_specs=[whole, whole, whole] + [whole] * first,
        scratch_shapes=[
            pltpu.VMEM((places, *block_shape), kind),
            pltpu.SemaphoreType.DMA((len(blocks) + 2,)),
        ],
        input_output_aliases={} if first else {len(operands) - 1: 0},
        compiler_params=pltpu.CompilerParams(vmem_limit_bytes=8 << 20),
        cost_estimate=pl.CostEstimate(
            flops=6 * 10 * 256 * 256 * 128, bytes_accessed=0,
            transcendentals=6 * 65536),
        name=("line_stage", "next_stage", "far_stage")[turn],
    )(*operands)


def wide(*parts):
    total = parts[0].astype(jnp.float32)
    for part in parts[1:]:
        total = total + part.astype(jnp.float32)
    return total


def add(*parts):
    return wide(*parts).astype(jnp.bfloat16)


def shards(queries, output_gradient, prefix_keys, prefix_values, tile_prefix, suffix_lse, suffix_dot):
    tile_count, row_count, _ = queries.shape
    dp = lax.axis_index("dp")
    pos = lax.axis_index("pos")

    own = spread(prefix_keys, prefix_values)
    line = exchange_line(own).reshape(SIDE, 256, 256)
    target = lax.dynamic_slice(tile_prefix, (dp * tile_count, 0), (tile_count, 1)).reshape(1, -1)
    far_z, far_y, far_core = target >> 3, target >> 1 & 3, target & 1
    near = jnp.where(far_core == 0, far_y, far_z)
    far = jnp.where(far_core == 0, (dp >> 3) - far_z, (dp >> 1 & 3) - far_y) & 3
    side = far_core ^ (dp & 1)
    next_one = far & 1
    at = side * (SIDE + SIDE * next_one) + next_one * (far >> 1) * SIDE + near
    code = target * 1024 + jnp.where(far == 0, 0, 2 - next_one) * 256 + at
    code = jnp.pad(code, ((0, 0), (0, 128 - tile_count)))
    sched = plan(code)

    def own_rows(x):
        x = jnp.transpose(x, (0, 2, 1))
        x = lax.dynamic_slice(
            x, (dp * tile_count, 0, pos * row_count), (tile_count, x.shape[1], row_count))
        return x.reshape(tile_count, 1, -1)

    stats = jnp.concatenate([own_rows(suffix_lse), own_rows(suffix_dot)], axis=1)

    line, sched, stats = lax.optimization_barrier((line, sched, stats))
    up, down = shift(line, 1), shift(line, -1)
    here, back = [], []

    def work(turn, block, tile_rows, query_grad):
        query_grad, sums, there, *rest = stage(turn, sched, tile_rows, stats, block, query_grad)
        here.append(sums)
        back.append(there)
        return query_grad, *rest

    def both(*block):
        return [*block, *map(swap_cores, block)]

    query_grad, tile_rows = work(0, both(line), (queries, output_gradient), None)
    up, down, query_grad = lax.optimization_barrier((up, down, query_grad))
    far = shift(up[0:2], 1), shift(down[2:4], -1)
    query_grad, = work(1, both(up, down), tile_rows, query_grad)
    far, query_grad = lax.optimization_barrier((far, query_grad))
    others = [swap_cores(x) for x in far]
    back[1], *others = lax.optimization_barrier((back[1], *others))
    query_grad, = work(2, [*far, *others], tile_rows, query_grad)
    back = [swap_cores(x) for x in back]

    to_up, to_down = add(here[1][0:4], back[1][0:4]), add(here[1][4:8], back[1][4:8])
    _, _, back[2] = lax.optimization_barrier((to_up, to_down, back[2]))
    from_up, from_down = shift(to_up, -1), shift(to_down, 1)
    from_far = shift(add(here[2][0:4], back[2]), 2)
    query_grad = settle(query_grad)
    near_sum, query_grad = lax.optimization_barrier(
        (wide(here[0][0:4], back[0], from_up, from_down), query_grad))
    line_sum = add(near_sum, from_far)
    total = add(*exchange_line(line_sum.reshape(own.shape)))
    return query_grad, total[None, :, 0:128], total[None, :, 128:256]


def solution(mesh):
    in_specs = (
        P("dp", "pos", "head"),
        P("dp", "pos", "head"),
        P("dp", "pos", "head"),
        P("dp", "pos", "head"),
        P(),
        P(None, None, "head"),
        P(None, None, "head"),
    )
    out_specs = (P("dp", "pos", "head"), P("dp", "pos", "head"), P("dp", "pos", "head"))
    return jax.shard_map(shards, mesh=mesh, in_specs=in_specs, out_specs=out_specs, check_vma=False)
```
